32 devices in a mesh: ctx: 8 (over y, x, core), wa: 4 (over z).
Axes of the slice: x: 2, y: 2, z: 4, core: 2. Of those that a mesh axis runs over, the one named last changes fastest.
Arguments:
- block_input: bfloat16 [4, 2048, 1024], P('wa', 'ctx'), may hold values from -6 to 6
- cotangent: bfloat16 [4, 2048, 1024], P('wa', 'ctx'), may hold values from -6 to 6
- pair_order: int32 [8], replicated, may hold values from 0 to 7, each once
- norm_gains: bfloat16 [2, 1024], P(None, ('ctx', 'wa')), may hold values from 0.099609375 to 1.8984375
- norm_biases: bfloat16 [2, 1024], P(None, ('ctx', 'wa')), may hold values from -3 to 3
- w_qkv: bfloat16 [1024, 3072], P(('ctx', 'wa')), may hold values from -0.1875 to 0.1875
- attn_bias: bfloat16 [2, 1024], P(None, ('ctx', 'wa')), may hold values from -3 to 3
- w_out: bfloat16 [1024, 1024], P(('ctx', 'wa')), may hold values from -2 to 2
- resid_biases: bfloat16 [2, 1024], P(None, ('ctx', 'wa')), may hold values from -3 to 3
- w_fc: bfloat16 [1024, 4096], P(('ctx', 'wa')), may hold values from -0.1875 to 0.1875
- fc_bias: bfloat16 [4096], P(('ctx', 'wa')), may hold values from -3 to 3
- w_proj: bfloat16 [4096, 1024], P(('ctx', 'wa')), may hold values from -0.09375 to 0.09375
Outputs:
- block_output: bfloat16 [4, 2048, 1024], P('wa', 'ctx')
- input_grad: float32 [4, 2048, 1024], P('wa', 'ctx')
- norm_gains_grad: float32 [2, 1024], P(None, ('ctx', 'wa'))
- norm_biases_grad: float32 [2, 1024], P(None, ('ctx', 'wa'))
- w_qkv_grad: float32 [1024, 3072], P(('ctx', 'wa'))
- attn_bias_grad: float32 [2, 1024], P(None, ('ctx', 'wa'))
- w_out_grad: float32 [1024, 1024], P(('ctx', 'wa'))
- resid_biases_grad: float32 [2, 1024], P(None, ('ctx', 'wa'))
- w_fc_grad: float32 [1024, 4096], P(('ctx', 'wa'))
- fc_bias_grad: float32 [4096], P(('ctx', 'wa'))
- w_proj_grad: float32 [4096, 1024], P(('ctx', 'wa'))
The draws below stay inside these ranges and needn't reach their ends.
Inputs may be any that keep to these rules, and one draw needn't show every extreme that they name: Index c of ctx holds causal blocks pair_order[c] and 15 - pair_order[c]; every value appears once.
All inputs are finite; a program needn't handle non-finite values.
Results may differ from the reference program's by a relative error of at most 0.025.
Values may be sent and summed in bfloat16 or wider, within the bound.
A program may use at most 192 MiB of HBM per device.

```python
import jax
import jax.numpy as jnp
from jax import lax

D = 1024
FF = 4096
HEADS = 16
HEAD_DIM = 64
BLK = 128
PAIRS = 8
ROWS = 2048
SEQS = 4
N_CTX = 8


def level_of(rng, dims, shards, low, high):
    loudness = 1.0
    for position, blocks in shards:
        heights = jax.random.uniform(jax.random.fold_in(jax.random.fold_in(rng, 6), position), (blocks,), jnp.float32, low / len(shards), high / len(shards))
        loudness = loudness * jnp.repeat(jnp.exp(heights), dims[position] // blocks).reshape((-1,) + (1,) * (len(dims) - 1 - position))
    return loudness


def scatter_about(key, extent, deviation, most, pieces=(), held_as=jnp.bfloat16):
    entries = jax.random.normal(key, extent, jnp.float32) * deviation
    if len(pieces) > 0:
        entries = level_of(key, extent, pieces, -0.22, 0.18) * entries
    return jnp.clip(entries, min=-most, max=most).astype(held_as)


def setup_inputs(seed: int = 0) -> dict:
    key_list = jax.random.split(jax.random.key(seed), 13)
    block_input = scatter_about(key_list[0], (SEQS, ROWS, D), 1.0, 6.0, ((0, 4), (1, 8)))
    cotangent = scatter_about(key_list[1], (SEQS, ROWS, D), 1.0, 6.0, ((0, 4), (1, 8)))
    pair_order = jax.random.permutation(key_list[2], PAIRS).astype(jnp.int32)
    norm_gains = jnp.clip(1.0 + 0.18 * jax.random.normal(key_list[3], (2, D), jnp.float32), 0.099609375, 1.8984375).astype(jnp.bfloat16)
    norm_biases = scatter_about(key_list[4], (2, D), 0.5, 3.0, ((1, 32),))
    w_qkv = scatter_about(key_list[5], (D, 3 * D), D ** -0.5, 0.1875, ((0, 32),))
    attn_bias = scatter_about(key_list[6], (2, D), 0.5, 3.0, ((1, 32),))
    w_out = scatter_about(key_list[7], (D, D), (max(1, 8 * D // (BLK * N_CTX))) ** -0.5, 2.0, ((0, 32),))
    resid_biases = scatter_about(key_list[8], (2, D), 0.5, 3.0, ((1, 32),))
    w_fc = scatter_about(key_list[9], (D, FF), D ** -0.5, 0.1875, ((0, 32),))
    fc_bias = scatter_about(key_list[10], (FF,), 0.5, 3.0, ((0, 32),))
    w_proj = scatter_about(key_list[11], (FF, D), FF ** -0.5, 0.09375, ((0, 32),))
    return dict(block_input=block_input, cotangent=cotangent, pair_order=pair_order, norm_gains=norm_gains, norm_biases=norm_biases, w_qkv=w_qkv, attn_bias=attn_bias, w_out=w_out, resid_biases=resid_biases, w_fc=w_fc, fc_bias=fc_bias, w_proj=w_proj)


@jax.custom_vjp
def low(v):
    return lax.optimization_barrier(v.astype(jnp.bfloat16)).astype(jnp.float32)

@jax.custom_vjp
def low_back(v):
    return v

def low_keep(v):
    return (low(v), None)

def low_pass(kept, grad):
    return (grad,)

def back_keep(v):
    return (v, None)

def back_low(kept, grad):
    return (low(grad),)
low.defvjp(low_keep, low_pass)
low_back.defvjp(back_keep, back_low)

def layer_norm(field, gain_row, shift_row):
    average = lax.optimization_barrier(jnp.mean(field, axis=-1, keepdims=True))
    centred = field - average
    variance = lax.optimization_barrier(jnp.mean(centred * centred, axis=-1, keepdims=True))
    return centred * lax.rsqrt(variance + 1e-05) * gain_row + shift_row

def gelu_tanh(field):
    return 0.5 * field * (1.0 + jnp.tanh(0.7978845608028654 * (field + 0.044715 * field * field * field)))

def matmul(left, right):
    return jnp.dot(left, right, precision=lax.Precision.HIGHEST)

def pair_positions(pair_order):
    pair_count = pair_order.shape[0]
    blocks = jnp.stack([pair_order, 2 * pair_count - 1 - pair_order], axis=1).astype(jnp.int32)
    inside = jnp.arange(BLK, dtype=jnp.int32)
    return (blocks[:, :, None] * BLK + inside[None, None, :]).reshape(-1).astype(jnp.int32)

def attend_rows(queries, key_rows, value_rows, query_positions, key_positions):
    scores = jnp.einsum('bhe,khe->hbk', queries, key_rows, precision=lax.Precision.HIGHEST) * 0.125
    scores = jnp.where(key_positions[None, None, :] <= query_positions[None, :, None], scores, -1e+30)
    scores = low_back(scores)
    log_total = jax.nn.logsumexp(scores, axis=-1, keepdims=True)
    probabilities = low(jnp.exp(scores - log_total))
    return jnp.einsum('hbk,khe->bhe', probabilities, value_rows, precision=lax.Precision.HIGHEST)

def forward(block_input, norm_gains, norm_biases, w_qkv, attn_bias, w_out, resid_biases, w_fc, fc_bias, w_proj, positions):
    seq_count, row_count, model_width = block_input.shape
    tokens = block_input.reshape(seq_count * row_count, model_width)
    first = low(layer_norm(tokens, norm_gains[0], norm_biases[0]))
    projected = matmul(first, w_qkv)
    queries = low_back(low(projected[:, :model_width] + attn_bias[0]))
    key_rows = low_back(low(projected[:, model_width:2 * model_width]))
    value_rows = low_back(low(projected[:, 2 * model_width:] + attn_bias[1]))
    head_shape = (seq_count, row_count, HEADS, HEAD_DIM)
    block_positions = positions.reshape(-1, 2 * BLK)

    def one_sequence(group):
        query_seq, key_seq, value_seq = group
        block_queries = query_seq.reshape(-1, 2 * BLK, HEADS, HEAD_DIM)

        def one_block(block_item):
            return attend_rows(block_item[0], key_seq, value_seq, block_item[1], positions)
        return lax.map(jax.checkpoint(one_block), (block_queries, block_positions)).reshape(query_seq.shape)
    attended = lax.map(one_sequence, (queries.reshape(head_shape), key_rows.reshape(head_shape), value_rows.reshape(head_shape)))
    attended = low_back(low(attended.reshape(seq_count * row_count, model_width)))
    branch = low_back(matmul(attended, w_out) + resid_biases[0])
    hidden = tokens + branch
    second = low(layer_norm(hidden, norm_gains[1], norm_biases[1]))
    pre_act = low_back(matmul(second, w_fc) + fc_bias)
    activation = low(gelu_tanh(pre_act))
    output = hidden + matmul(activation, w_proj) + resid_biases[1]
    return output.reshape(seq_count, row_count, model_width)

def reference(block_input, cotangent, pair_order, norm_gains, norm_biases, w_qkv, attn_bias, w_out, resid_biases, w_fc, fc_bias, w_proj):
    positions = pair_positions(pair_order)
    inputs = tuple((argument.astype(jnp.float32) for argument in (block_input, norm_gains, norm_biases, w_qkv, attn_bias, w_out, resid_biases, w_fc, fc_bias, w_proj)))

    def wrapped(*arrays):
        return forward(*arrays, positions)
    output, pull = jax.vjp(wrapped, *inputs)
    grads = pull(cotangent.astype(jnp.float32))
    return (output.astype(jnp.bfloat16), grads[0], grads[1], grads[2], grads[3], grads[4], grads[5], grads[6], grads[7], grads[8], grads[9])
```

```python
import functools

import jax
import jax.numpy as jnp
from jax import lax
from jax.experimental import pallas as pl
from jax.experimental.pallas import tpu as pltpu
from jax.sharding import PartitionSpec as P

HEAD_DIM = 64
EPSILON = 1e-05
TILE = 256
BOTH = ("ctx", "wa")
LOW = jnp.bfloat16
WIDE = jnp.float32


def normalize(field):
    average = jnp.mean(field, axis=-1, keepdims=True)
    centred = field - average
    variance = jnp.mean(centred * centred, axis=-1, keepdims=True)
    factor = lax.rsqrt(variance + EPSILON)
    return (centred * factor, factor)


def norm_back(grad_normed, normed, factor):
    return factor * (
        grad_normed
        - jnp.mean(grad_normed, axis=-1, keepdims=True)
        - normed * jnp.mean(grad_normed * normed, axis=-1, keepdims=True)
    )


def gelu_tanh(field):
    return (
        0.5
        * field
        * (1.0 + jnp.tanh(0.7978845608028654 * (field + 0.044715 * field * field * field)))
    )


def contract(left, right, left_dim, right_dim):
    return lax.dot_general(
        left, right, (((left_dim,), (right_dim,)), ((), ())), preferred_element_type=WIDE
    )


def causal(shape):
    keys = lax.broadcasted_iota(jnp.int32, shape, 0)
    rows = lax.broadcasted_iota(jnp.int32, shape, 1)
    return keys <= rows


def unpack(where_ref, source_ref, targets, block, scales):
    count = source_ref.shape[0] // block
    heads = targets[0].shape[0]

    def one(index, carried):
        rows = source_ref[pl.ds(pl.multiple_of(where_ref[index] * block, block), block), :]
        place = pl.ds(pl.multiple_of(index * block, block), block)
        for part, (target, scale) in enumerate(zip(targets, scales)):
            for head in range(heads):
                start = (part * heads + head) * HEAD_DIM
                piece = rows[:, start : start + HEAD_DIM]
                if scale != 1.0:
                    piece = (piece.astype(WIDE) * scale).astype(LOW)
                target[head, place, :] = piece
        return carried

    lax.fori_loop(0, count, one, 0)


def attend_kernel(block, where_ref, qkv_ref, out_ref, log_ref, q_s, k_s, v_s):
    step = pl.program_id(0)
    heads = q_s.shape[0]

    @pl.when(step == 0)
    def _():
        unpack(where_ref, qkv_ref, (q_s, k_s, v_s), block, (0.125, 1.0, 1.0))

    here = pl.ds(pl.multiple_of(step * TILE, TILE), TILE)
    queries = [q_s[head, here, :] for head in range(heads)]

    def visit(keys_at, state, masked):
        out = []
        for head in range(heads):
            top, total, summed = state[head]
            scores = contract(k_s[head, keys_at, :], queries[head], 1, 1)
            if masked:
                scores = jnp.where(causal(scores.shape), scores, -1e30)
            new_top = jnp.maximum(top, jnp.max(scores, axis=0, keepdims=True))
            weights = jnp.exp(scores - new_top)
            shrink = jnp.exp(top - new_top)
            total = total * shrink + jnp.sum(weights, axis=0, keepdims=True)
            summed = summed * shrink + contract(
                v_s[head, keys_at, :], weights.astype(LOW), 0, 0
            )
            out.append((new_top, total, summed))
        return tuple(out)

    start = tuple(
        (
            jnp.full((1, TILE), -1e30, WIDE),
            jnp.zeros((1, TILE), WIDE),
            jnp.zeros((HEAD_DIM, TILE), WIDE),
        )
        for _ in range(heads)
    )
    state = lax.fori_loop(
        0,
        step,
        lambda j, carried: visit(pl.ds(pl.multiple_of(j * TILE, TILE), TILE), carried, False),
        start,
    )
    state = visit(here, state, True)
    pieces = []
    for head in range(heads):
        top, total, summed = state[head]
        log_ref[step, head : head + 1, :] = top + jnp.log(total)
        pieces.append((summed / total).T)
    rows = jnp.concatenate(pieces, axis=1).astype(LOW) if heads > 1 else pieces[0].astype(LOW)
    per = TILE // block
    for part in range(per):
        place = pl.multiple_of(where_ref[step * per + part] * block, block)
        out_ref[pl.ds(place, block), :] = rows[part * block : (part + 1) * block, :]


def attend(where, qkv, block):
    rows, width = qkv.shape[0], qkv.shape[1] // 3
    heads = width // HEAD_DIM
    tiles = rows // TILE
    held = pltpu.VMEM((heads, rows, HEAD_DIM), LOW)
    return pl.pallas_call(
        functools.partial(attend_kernel, block),
        grid=(tiles,),
        out_shape=(
            jax.ShapeDtypeStruct((rows, width), LOW),
            jax.ShapeDtypeStruct((tiles, heads, TILE), WIDE),
        ),
        in_specs=[
            pl.BlockSpec(memory_space=pltpu.SMEM),
            pl.BlockSpec((rows, 3 * width), lambda i: (0, 0)),
        ],
        out_specs=(
            pl.BlockSpec((rows, width), lambda i: (0, 0)),
            pl.BlockSpec((tiles, heads, TILE), lambda i: (0, 0, 0)),
        ),
        scratch_shapes=[held, held, held],
        compiler_params=pltpu.CompilerParams(vmem_limit_bytes=48 << 20),
        cost_estimate=pl.CostEstimate(
            flops=2 * rows * rows * 2 * width,
            bytes_accessed=rows * width * 8,
            transcendentals=rows * rows * heads // 2,
        ),
        name="attend",
    )(where, qkv)


def attend_back_kernel(
    block,
    where_ref,
    qkv_ref,
    attended_ref,
    grad_ref,
    log_ref,
    out_ref,
    q_s,
    k_s,
    v_s,
    a_s,
    g_s,
    dq_s,
    delta_s,
):
    step = pl.program_id(0)
    tiles = pl.num_programs(0)
    heads = q_s.shape[0]
    width = heads * HEAD_DIM

    @pl.when(step == 0)
    def _():
        unpack(where_ref, qkv_ref, (q_s, k_s, v_s), block, (0.125, 1.0, 1.0))
        unpack(where_ref, attended_ref, (a_s,), block, (1.0,))
        unpack(where_ref, grad_ref, (g_s,), block, (1.0,))
        dq_s[...] = jnp.zeros_like(dq_s)

        def one(index, carried):
            place = pl.ds(pl.multiple_of(index * TILE, TILE), TILE)
            for head in range(heads):
                product = a_s[head, place, :].astype(WIDE) * g_s[head, place, :].astype(WIDE)
                delta_s[index, head : head + 1, :] = jnp.sum(product.T, axis=0, keepdims=True)
            return carried

        lax.fori_loop(0, delta_s.shape[0], one, 0)

    here = pl.ds(pl.multiple_of(step * TILE, TILE), TILE)
    keys = [k_s[head, here, :] for head in range(heads)]
    values = [v_s[head, here, :] for head in range(heads)]

    def visit(index, state, masked):
        place = pl.ds(pl.multiple_of(index * TILE, TILE), TILE)
        out = []
        for head in range(heads):
            dk, dv = state[head]
            queries = q_s[head, place, :]
            grads = g_s[head, place, :]
            scores = contract(keys[head], queries, 1, 1)
            if masked:
                scores = jnp.where(causal(scores.shape), scores, -1e30)
            weights = jnp.exp(scores - log_ref[index, head : head + 1, :])
            pulled = contract(values[head], grads, 1, 1)
            score_grad = (weights * (pulled - delta_s[index, head : head + 1, :])).astype(LOW)
            dv = dv + contract(weights.astype(LOW), grads, 1, 0)
            dk = dk + contract(score_grad, queries, 1, 0)
            dq_s[head, place, :] += contract(score_grad, keys[head], 0, 0)
            out.append((dk, dv))
        return tuple(out)

    zero = jnp.zeros((TILE, HEAD_DIM), WIDE)
    state = visit(step, tuple((zero, zero) for _ in range(heads)), True)
    state = lax.fori_loop(step + 1, tiles, lambda i, carried: visit(i, carried, False), state)
    pieces = [dq_s[head, here, :] * 0.125 for head in range(heads)]
    pieces += [state[head][0] for head in range(heads)]
    pieces += [state[head][1] for head in range(heads)]
    rows = jnp.concatenate(pieces, axis=1).astype(LOW)
    per = TILE // block
    for part in range(per):
        place = pl.multiple_of(where_ref[step * per + part] * block, block)
        out_ref[pl.ds(place, block), :] = rows[part * block : (part + 1) * block, :]


def attend_back(where, qkv, attended, grad, logs, block):
    rows, width = attended.shape
    heads = width // HEAD_DIM
    tiles = rows // TILE
    held = pltpu.VMEM((heads, rows, HEAD_DIM), LOW)

    def whole(*shape):
        return pl.BlockSpec(shape, lambda i: (0,) * len(shape))

    return pl.pallas_call(
        functools.partial(attend_back_kernel, block),
        grid=(tiles,),
        out_shape=jax.ShapeDtypeStruct((rows, 3 * width), LOW),
        in_specs=[
            pl.BlockSpec(memory_space=pltpu.SMEM),
            whole(rows, 3 * width),
            whole(rows, width),
            whole(rows, width),
            whole(tiles, heads, TILE),
        ],
        out_specs=whole(rows, 3 * width),
        scratch_shapes=[
            held,
            held,
            held,
            held,
            held,
            pltpu.VMEM((heads, rows, HEAD_DIM), WIDE),
            pltpu.VMEM((tiles, heads, TILE), WIDE),
        ],
        compiler_params=pltpu.CompilerParams(vmem_limit_bytes=56 << 20),
        cost_estimate=pl.CostEstimate(
            flops=5 * rows * rows * 2 * width,
            bytes_accessed=rows * width * 16,
            transcendentals=rows * rows * heads // 2,
        ),
        name="attend_back",
    )(where, qkv, attended, grad, logs)


def gather_rows(rows):
    return lax.all_gather(rows, "ctx", axis=0, tiled=True)


def scatter_rows(partial):
    return lax.psum_scatter(partial, "ctx", scatter_dimension=0, tiled=True).astype(WIDE)


def on_device(
    block_input,
    cotangent,
    pair_order,
    norm_gains,
    norm_biases,
    w_qkv,
    attn_bias,
    w_out,
    resid_biases,
    w_fc,
    fc_bias,
    w_proj,
):
    ctx_count = lax.axis_size("ctx")
    wa_count = lax.axis_size("wa")
    device_count = ctx_count * wa_count
    ctx_index = lax.axis_index("ctx")
    wa_index = lax.axis_index("wa")
    tokens = block_input[0].astype(WIDE)
    row_count, model_width = tokens.shape
    block = row_count // 2
    share = model_width // device_count
    hidden_share = fc_bias.shape[0]
    width = model_width // ctx_count
    hidden_width = hidden_share * wa_count
    depth = w_qkv.shape[0]

    blocks = jnp.stack([pair_order, 2 * ctx_count - 1 - pair_order], axis=1).reshape(-1)
    numbers = jnp.arange(2 * ctx_count, dtype=jnp.int32)
    where = jnp.sum(
        jnp.where(blocks[None, :] == numbers[:, None], numbers[None, :], 0), axis=1
    ).astype(jnp.int32)

    small = jnp.concatenate(
        [
            norm_gains.reshape(-1),
            norm_biases.reshape(-1),
            attn_bias.reshape(-1),
            resid_biases.reshape(-1),
            fc_bias,
        ]
    )[None]
    small_all = lax.all_gather(small, BOTH, axis=0, tiled=True).astype(WIDE)

    def rows_of(part):
        piece = small_all[:, part * 2 * share : (part + 1) * 2 * share]
        return piece.reshape(device_count, 2, share).transpose(1, 0, 2).reshape(2, model_width)

    gains, shifts, qv_bias, out_bias = (rows_of(part) for part in range(4))
    qv_own = lax.dynamic_slice_in_dim(qv_bias, ctx_index * width, width, axis=1)
    fc_own = lax.dynamic_slice_in_dim(
        small_all[:, 8 * share :], ctx_index * wa_count, wa_count, axis=0
    ).reshape(hidden_width)

    qkv_cut = w_qkv.reshape(depth, 3, ctx_count, width).transpose(2, 0, 1, 3)
    qkv_cut = qkv_cut.reshape(ctx_count, depth, 3 * width)
    qkv_cut = lax.all_to_all(qkv_cut, "ctx", 0, 0, tiled=True)
    qkv_own = lax.all_gather(qkv_cut, "wa", axis=1, tiled=True).reshape(model_width, 3 * width)
    out_own = lax.all_gather(w_out, "wa", axis=0, tiled=True)
    fc_cut = w_fc.reshape(depth, ctx_count, hidden_width).transpose(1, 0, 2)
    fc_cut = lax.all_to_all(fc_cut, "ctx", 0, 0, tiled=True)
    fc_mat = lax.all_gather(fc_cut, "wa", axis=1, tiled=True).reshape(model_width, hidden_width)
    proj_own = lax.all_gather(w_proj, "wa", axis=0, tiled=True)

    first_normed, first_factor = normalize(tokens)
    first = gather_rows((first_normed * gains[0] + shifts[0]).astype(LOW))
    qkv_bias = jnp.concatenate([qv_own[0], jnp.zeros((width,), WIDE), qv_own[1]])
    qkv = (jnp.dot(first, qkv_own, preferred_element_type=WIDE) + qkv_bias).astype(LOW)
    attended, logs = attend(where, qkv, block)
    branch = scatter_rows(jnp.dot(attended, out_own, preferred_element_type=WIDE).astype(LOW))
    hidden = tokens + branch + out_bias[0]

    second_normed, second_factor = normalize(hidden)
    second = gather_rows((second_normed * gains[1] + shifts[1]).astype(LOW))
    pre_act = jnp.dot(second, fc_mat, preferred_element_type=WIDE) + fc_own
    activation, gelu_pull = jax.vjp(gelu_tanh, pre_act)
    activation_low = activation.astype(LOW)
    grad_out = cotangent[0]
    grad_wide = grad_out.astype(WIDE)
    grad_all = gather_rows(grad_out)
    act_grad = contract(grad_all, proj_own, 1, 1)
    pre_grad = gelu_pull(act_grad)[0].astype(LOW)
    second_grad = scatter_rows(contract(pre_grad, fc_mat, 1, 1).astype(LOW))
    output = (
        hidden
        + scatter_rows(jnp.dot(activation_low, proj_own, preferred_element_type=WIDE).astype(LOW))
        + out_bias[1]
    )

    proj_grad = contract(activation_low, grad_all, 0, 0).astype(LOW)
    proj_sum = lax.psum_scatter(proj_grad, "wa", scatter_dimension=0, tiled=True).astype(WIDE)
    fc_grad = contract(second, pre_grad, 0, 0).astype(LOW)
    fc_grad = fc_grad.reshape(ctx_count, wa_count * depth, hidden_width)
    fc_sum = lax.psum_scatter(fc_grad, "wa", scatter_dimension=1, tiled=True)
    fc_sum = lax.all_to_all(fc_sum, "ctx", 0, 0, tiled=True)
    fc_sum = fc_sum.transpose(1, 0, 2).reshape(depth, -1).astype(WIDE)
    fc_bias_grad = jnp.sum(pre_grad.astype(WIDE), axis=0)

    gain_two = jnp.sum(second_grad * second_normed, axis=0)
    shift_two = jnp.sum(second_grad, axis=0)
    hidden_grad = grad_wide + norm_back(second_grad * gains[1], second_normed, second_factor)
    branch_low = hidden_grad.astype(LOW)
    branch_grad = gather_rows(branch_low)
    attended_grad = contract(branch_grad, out_own, 1, 1).astype(LOW)
    qkv_grad = attend_back(where, qkv, attended, attended_grad, logs, block)
    first_grad = scatter_rows(contract(qkv_grad, qkv_own, 1, 1).astype(LOW))

    out_grad = contract(attended, branch_grad, 0, 0).astype(LOW)
    out_sum = lax.psum_scatter(out_grad, "wa", scatter_dimension=0, tiled=True).astype(WIDE)
    weight_grad = contract(first, qkv_grad, 0, 0).astype(LOW)
    weight_grad = weight_grad.reshape(ctx_count, wa_count * depth, 3 * width)
    qkv_sum = lax.psum_scatter(weight_grad, "wa", scatter_dimension=1, tiled=True)
    qkv_sum = lax.all_to_all(qkv_sum, "ctx", 0, 0, tiled=True)
    qkv_sum = qkv_sum.reshape(ctx_count, depth, 3, width).transpose(1, 2, 0, 3)
    qkv_sum = qkv_sum.reshape(depth, 3 * model_width).astype(WIDE)
    qkv_bias_grad = jnp.sum(qkv_grad.astype(WIDE), axis=0)

    gain_one = jnp.sum(first_grad * first_normed, axis=0)
    shift_one = jnp.sum(first_grad, axis=0)
    input_grad = hidden_grad + norm_back(first_grad * gains[0], first_normed, first_factor)

    own = (lax.broadcasted_iota(jnp.int32, (ctx_count, 1), 0) == ctx_index).astype(WIDE)

    def spread(row):
        return (own * row[None]).reshape(-1)

    pairs = [
        gain_one,
        gain_two,
        shift_one,
        shift_two,
        spread(qkv_bias_grad[:width]),
        spread(qkv_bias_grad[2 * width :]),
        jnp.sum(branch_low.astype(WIDE), axis=0),
        jnp.sum(grad_wide, axis=0),
    ]
    owned = jnp.concatenate(
        [row.reshape(device_count, share) for row in pairs]
        + [spread(fc_bias_grad).reshape(device_count, hidden_share)],
        axis=1,
    )
    summed = lax.psum(owned, BOTH)
    mine = lax.dynamic_slice_in_dim(summed, ctx_index * wa_count + wa_index, 1, axis=0)[0]
    small_grads = [
        mine[part * 2 * share : (part + 1) * 2 * share].reshape(2, share) for part in range(4)
    ]
    return (
        output.astype(LOW)[None],
        input_grad[None],
        small_grads[0],
        small_grads[1],
        qkv_sum,
        small_grads[2],
        out_sum,
        small_grads[3],
        fc_sum,
        mine[8 * share :],
        proj_sum,
    )


def solution(mesh):
    rows = P("wa", "ctx", None)
    first_dim = P(BOTH, None)
    second_dim = P(None, BOTH)
    return jax.shard_map(
        on_device,
        mesh=mesh,
        in_specs=(
            rows,
            rows,
            P(),
            second_dim,
            second_dim,
            first_dim,
            second_dim,
            first_dim,
            second_dim,
            first_dim,
            P(BOTH),
            first_dim,
        ),
        out_specs=(
            rows,
            rows,
            second_dim,
            second_dim,
            first_dim,
            second_dim,
            first_dim,
            second_dim,
            first_dim,
            P(BOTH),
            first_dim,
        ),
        check_vma=False,
    )
```

```python
import functools

import jax
import jax.numpy as jnp
from jax import lax
from jax.experimental import pallas as pl
from jax.experimental.pallas import tpu as pltpu
from jax.sharding import PartitionSpec as P

HEAD_DIM = 64
EPSILON = 1e-05
TILE = 256
BOTH = ("ctx", "wa")
LOW = jnp.bfloat16
WIDE = jnp.float32
MESH = pl.DeviceIdType.MESH


def normalize(field):
    average = jnp.mean(field, axis=-1, keepdims=True)
    centred = field - average
    variance = jnp.mean(centred * centred, axis=-1, keepdims=True)
    factor = lax.rsqrt(variance + EPSILON)
    return (centred * factor, factor)


def norm_back(grad_normed, normed, factor):
    return factor * (
        grad_normed
        - jnp.mean(grad_normed, axis=-1, keepdims=True)
        - normed * jnp.mean(grad_normed * normed, axis=-1, keepdims=True)
    )


def gelu_tanh(field):
    return (
        0.5
        * field
        * (1.0 + jnp.tanh(0.7978845608028654 * (field + 0.044715 * field * field * field)))
    )


def contract(left, right, left_dim, right_dim):
    return lax.dot_general(
        left, right, (((left_dim,), (right_dim,)), ((), ())), preferred_element_type=WIDE
    )


def causal(shape):
    keys = lax.broadcasted_iota(jnp.int32, shape, 0)
    rows = lax.broadcasted_iota(jnp.int32, shape, 1)
    return keys <= rows


def unpack(where_ref, source_ref, targets, block, scales):
    count = source_ref.shape[0] // block
    heads = targets[0].shape[0]

    def one(index, carried):
        rows = source_ref[pl.ds(pl.multiple_of(where_ref[index] * block, block), block), :]
        place = pl.ds(pl.multiple_of(index * block, block), block)
        for part, (target, scale) in enumerate(zip(targets, scales)):
            for head in range(heads):
                start = (part * heads + head) * HEAD_DIM
                piece = rows[:, start : start + HEAD_DIM]
                if scale != 1.0:
                    piece = (piece.astype(WIDE) * scale).astype(LOW)
                target[head, place, :] = piece
        return carried

    lax.fori_loop(0, count, one, 0)


def attend_kernel(block, where_ref, qkv_ref, out_ref, log_ref, q_s, k_s, v_s):
    step = pl.program_id(0)
    heads = q_s.shape[0]

    @pl.when(step == 0)
    def _():
        unpack(where_ref, qkv_ref, (q_s, k_s, v_s), block, (0.125, 1.0, 1.0))

    here = pl.ds(pl.multiple_of(step * TILE, TILE), TILE)
    queries = [q_s[head, here, :] for head in range(heads)]

    def visit(keys_at, state, masked):
        out = []
        for head in range(heads):
            top, total, summed = state[head]
            scores = contract(k_s[head, keys_at, :], queries[head], 1, 1)
            if masked:
                scores = jnp.where(causal(scores.shape), scores, -1e30)
            new_top = jnp.maximum(top, jnp.max(scores, axis=0, keepdims=True))
            weights = jnp.exp(scores - new_top)
            shrink = jnp.exp(top - new_top)
            total = total * shrink + jnp.sum(weights, axis=0, keepdims=True)
            summed = summed * shrink + contract(
                v_s[head, keys_at, :], weights.astype(LOW), 0, 0
            )
            out.append((new_top, total, summed))
        return tuple(out)

    start = tuple(
        (
            jnp.full((1, TILE), -1e30, WIDE),
            jnp.zeros((1, TILE), WIDE),
            jnp.zeros((HEAD_DIM, TILE), WIDE),
        )
        for _ in range(heads)
    )
    state = lax.fori_loop(
        0,
        step,
        lambda j, carried: visit(pl.ds(pl.multiple_of(j * TILE, TILE), TILE), carried, False),
        start,
    )
    state = visit(here, state, True)
    pieces = []
    for head in range(heads):
        top, total, summed = state[head]
        log_ref[step, head : head + 1, :] = top + jnp.log(total)
        pieces.append((summed / total).T)
    rows = jnp.concatenate(pieces, axis=1).astype(LOW) if heads > 1 else pieces[0].astype(LOW)
    per = TILE // block
    for part in range(per):
        place = pl.multiple_of(where_ref[step * per + part] * block, block)
        out_ref[pl.ds(place, block), :] = rows[part * block : (part + 1) * block, :]


def attend(where, qkv, block):
    rows, width = qkv.shape[0], qkv.shape[1] // 3
    heads = width // HEAD_DIM
    tiles = rows // TILE
    held = pltpu.VMEM((heads, rows, HEAD_DIM), LOW)
    return pl.pallas_call(
        functools.partial(attend_kernel, block),
        grid=(tiles,),
        out_shape=(
            jax.ShapeDtypeStruct((rows, width), LOW),
            jax.ShapeDtypeStruct((tiles, heads, TILE), WIDE),
        ),
        in_specs=[
            pl.BlockSpec(memory_space=pltpu.SMEM),
            pl.BlockSpec((rows, 3 * width), lambda i: (0, 0)),
        ],
        out_specs=(
            pl.BlockSpec((rows, width), lambda i: (0, 0)),
            pl.BlockSpec((tiles, heads, TILE), lambda i: (0, 0, 0)),
        ),
        scratch_shapes=[held, held, held],
        compiler_params=pltpu.CompilerParams(vmem_limit_bytes=48 << 20),
        cost_estimate=pl.CostEstimate(
            flops=2 * rows * rows * 2 * width,
            bytes_accessed=rows * width * 8,
            transcendentals=rows * rows * heads // 2,
        ),
        name="attend",
    )(where, qkv)


def attend_back_kernel(
    block,
    where_ref,
    qkv_ref,
    attended_ref,
    grad_ref,
    log_ref,
    out_ref,
    q_s,
    k_s,
    v_s,
    a_s,
    g_s,
    dq_s,
    delta_s,
):
    step = pl.program_id(0)
    tiles = pl.num_programs(0)
    heads = q_s.shape[0]
    width = heads * HEAD_DIM

    @pl.when(step == 0)
    def _():
        unpack(where_ref, qkv_ref, (q_s, k_s, v_s), block, (0.125, 1.0, 1.0))
        unpack(where_ref, attended_ref, (a_s,), block, (1.0,))
        unpack(where_ref, grad_ref, (g_s,), block, (1.0,))
        dq_s[...] = jnp.zeros_like(dq_s)

        def one(index, carried):
            place = pl.ds(pl.multiple_of(index * TILE, TILE), TILE)
            for head in range(heads):
                product = a_s[head, place, :].astype(WIDE) * g_s[head, place, :].astype(WIDE)
                delta_s[index, head : head + 1, :] = jnp.sum(product.T, axis=0, keepdims=True)
            return carried

        lax.fori_loop(0, delta_s.shape[0], one, 0)

    here = pl.ds(pl.multiple_of(step * TILE, TILE), TILE)
    keys = [k_s[head, here, :] for head in range(heads)]
    values = [v_s[head, here, :] for head in range(heads)]

    def visit(index, state, masked):
        place = pl.ds(pl.multiple_of(index * TILE, TILE), TILE)
        out = []
        for head in range(heads):
            dk, dv = state[head]
            queries = q_s[head, place, :]
            grads = g_s[head, place, :]
            scores = contract(keys[head], queries, 1, 1)
            if masked:
                scores = jnp.where(causal(scores.shape), scores, -1e30)
            weights = jnp.exp(scores - log_ref[index, head : head + 1, :])
            pulled = contract(values[head], grads, 1, 1)
            score_grad = (weights * (pulled - delta_s[index, head : head + 1, :])).astype(LOW)
            dv = dv + contract(weights.astype(LOW), grads, 1, 0)
            dk = dk + contract(score_grad, queries, 1, 0)
            dq_s[head, place, :] += contract(score_grad, keys[head], 0, 0)
            out.append((dk, dv))
        return tuple(out)

    zero = jnp.zeros((TILE, HEAD_DIM), WIDE)
    state = visit(step, tuple((zero, zero) for _ in range(heads)), True)
    state = lax.fori_loop(step + 1, tiles, lambda i, carried: visit(i, carried, False), state)
    pieces = [dq_s[head, here, :] * 0.125 for head in range(heads)]
    pieces += [state[head][0] for head in range(heads)]
    pieces += [state[head][1] for head in range(heads)]
    rows = jnp.concatenate(pieces, axis=1).astype(LOW)
    per = TILE // block
    for part in range(per):
        place = pl.multiple_of(where_ref[step * per + part] * block, block)
        out_ref[pl.ds(place, block), :] = rows[part * block : (part + 1) * block, :]


def attend_back(where, qkv, attended, grad, logs, block):
    rows, width = attended.shape
    heads = width // HEAD_DIM
    tiles = rows // TILE
    held = pltpu.VMEM((heads, rows, HEAD_DIM), LOW)

    def whole(*shape):
        return pl.BlockSpec(shape, lambda i: (0,) * len(shape))

    return pl.pallas_call(
        functools.partial(attend_back_kernel, block),
        grid=(tiles,),
        out_shape=jax.ShapeDtypeStruct((rows, 3 * width), LOW),
        in_specs=[
            pl.BlockSpec(memory_space=pltpu.SMEM),
            whole(rows, 3 * width),
            whole(rows, width),
            whole(rows, width),
            whole(tiles, heads, TILE),
        ],
        out_specs=whole(rows, 3 * width),
        scratch_shapes=[
            held,
            held,
            held,
            held,
            held,
            pltpu.VMEM((heads, rows, HEAD_DIM), WIDE),
            pltpu.VMEM((tiles, heads, TILE), WIDE),
        ],
        compiler_params=pltpu.CompilerParams(vmem_limit_bytes=56 << 20),
        cost_estimate=pl.CostEstimate(
            flops=5 * rows * rows * 2 * width,
            bytes_accessed=rows * width * 16,
            transcendentals=rows * rows * heads // 2,
        ),
        name="attend_back",
    )(where, qkv, attended, grad, logs)


def gather_rows(rows):
    return lax.all_gather(rows, "ctx", axis=0, tiled=True)


def greet(partners):
    barrier = pltpu.get_barrier_semaphore()
    for partner in partners:
        pl.semaphore_signal(barrier, inc=1, device_id=partner, device_id_type=MESH)
    pl.semaphore_wait(barrier, len(partners))


def remote(source, target, send, receive, partner):
    return pltpu.make_async_remote_copy(
        src_ref=source,
        dst_ref=target,
        send_sem=send,
        recv_sem=receive,
        device_id=partner,
        device_id_type=MESH,
    )


def scatter_kernel(
    count,
    partial_ref,
    out_ref,
    held,
    near,
    leaving,
    far,
    load_sem,
    near_send,
    near_recv,
    far_send,
    far_recv,
):
    chips = count // 2
    me = lax.axis_index("ctx")
    chip, core = me // 2, me % 2
    sibling = {"ctx": 2 * chip + 1 - core}
    places = [(chip + k) % chips for k in range(chips)]
    peers = [{"ctx": 2 * place + core} for place in places]
    loads, nears = {}, {}
    order = list(range(1, chips)) + [0]
    for k in order:
        loads[k] = pltpu.make_async_copy(
            partial_ref.at[2 * places[k] + core], held.at[k], load_sem.at[k]
        )
        loads[k].start()
    greet([sibling] + peers[1:])
    for k in order:
        nears[k] = remote(
            partial_ref.at[2 * places[k] + 1 - core],
            near.at[k],
            near_send.at[k],
            near_recv.at[k],
            sibling,
        )
        nears[k].start()
    fars = {}
    for k in range(1, chips):
        loads[k].wait()
        nears[k].wait_recv()
        leaving[k] = (held[k].astype(WIDE) + near[k].astype(WIDE)).astype(LOW)
        fars[k] = remote(
            leaving.at[k], far.at[chips - k], far_send.at[k], far_recv.at[chips - k], peers[k]
        )
        fars[k].start()
    loads[0].wait()
    nears[0].wait_recv()
    out_ref[...] = held[0].astype(WIDE) + near[0].astype(WIDE)
    for k in range(1, chips):
        fars[k].wait_recv()
        out_ref[...] += far[chips - k].astype(WIDE)
    for k in order:
        nears[k].wait_send()
    for k in range(1, chips):
        fars[k].wait_send()


def scatter_rows(partial):
    count = lax.axis_size("ctx")
    chips = count // 2
    rows, columns = partial.shape[0] // count, partial.shape[1]
    slots = pltpu.VMEM((chips, rows, columns), LOW)
    sems = pltpu.SemaphoreType.DMA((chips,))
    return pl.pallas_call(
        functools.partial(scatter_kernel, count),
        out_shape=jax.ShapeDtypeStruct((rows, columns), WIDE),
        in_specs=[pl.BlockSpec(memory_space=pl.ANY)],
        out_specs=pl.BlockSpec(memory_space=pltpu.VMEM),
        scratch_shapes=[slots] * 4 + [sems] * 5,
        compiler_params=pltpu.CompilerParams(
            collective_id=2, has_side_effects=True, vmem_limit_bytes=40 << 20
        ),
        cost_estimate=pl.CostEstimate(
            flops=count * rows * columns,
            bytes_accessed=40 * count * rows * columns,
            transcendentals=0,
        ),
        name="scatter_rows",
    )(partial.reshape(count, rows, columns))


def small_gather_kernel(ctx_count, wa_count, in_ref, out_ref, a_send, a_recv, b_send, b_recv):
    ctx, wa = lax.axis_index("ctx"), lax.axis_index("wa")
    along = [{"wa": (wa + k) % wa_count} for k in range(1, wa_count)]
    across = [{"ctx": (ctx + k) % ctx_count} for k in range(1, ctx_count)]
    greet(along + across)
    out_ref[ctx, wa] = in_ref[...]
    copies = [
        remote(in_ref, out_ref.at[ctx, wa], a_send.at[k], a_recv.at[k], partner)
        for k, partner in enumerate(along)
    ]
    for copy in copies:
        copy.start()
    for copy in copies:
        copy.wait()
    copies = [
        remote(out_ref.at[ctx], out_ref.at[ctx], b_send.at[k], b_recv.at[k], partner)
        for k, partner in enumerate(across)
    ]
    for copy in copies:
        copy.start()
    for copy in copies:
        copy.wait()


def small_gather(rows):
    ctx_count, wa_count = lax.axis_size("ctx"), lax.axis_size("wa")
    a_sems = pltpu.SemaphoreType.DMA((wa_count - 1,))
    b_sems = pltpu.SemaphoreType.DMA((ctx_count - 1,))
    return pl.pallas_call(
        functools.partial(small_gather_kernel, ctx_count, wa_count),
        out_shape=jax.ShapeDtypeStruct((ctx_count, wa_count) + rows.shape, WIDE),
        in_specs=[pl.BlockSpec(memory_space=pltpu.VMEM)],
        out_specs=pl.BlockSpec(memory_space=pltpu.VMEM),
        scratch_shapes=[a_sems, a_sems, b_sems, b_sems],
        compiler_params=pltpu.CompilerParams(collective_id=0, has_side_effects=True),
        name="small_gather",
    )(rows)


def small_sum_kernel(
    ctx_count, wa_count, in_ref, out_ref, a_s, mid_s, b_s, a_send, a_recv, b_send, b_recv
):
    ctx, wa = lax.axis_index("ctx"), lax.axis_index("wa")
    greet(
        [{"wa": (wa + k) % wa_count} for k in range(1, wa_count)]
        + [{"ctx": (ctx + k) % ctx_count} for k in range(1, ctx_count)]
    )
    copies = []
    for k in range(1, ctx_count):
        place = (ctx + k) % ctx_count
        copies.append(
            remote(in_ref.at[place], a_s.at[k], a_send.at[k], a_recv.at[k], {"ctx": place})
        )
        copies[-1].start()
    total = in_ref[ctx]
    for k in range(1, ctx_count):
        copies[k - 1].wait()
        total = total + a_s[k]
    mid_s[...] = total
    copies = []
    for k in range(1, wa_count):
        place = (wa + k) % wa_count
        copies.append(
            remote(mid_s.at[place], b_s.at[k], b_send.at[k], b_recv.at[k], {"wa": place})
        )
        copies[-1].start()
    total = mid_s[wa]
    for k in range(1, wa_count):
        copies[k - 1].wait()
        total = total + b_s[k]
    out_ref[...] = total


def small_sum(parts):
    ctx_count, wa_count = parts.shape[:2]
    inner = parts.shape[1:]
    a_sems = pltpu.SemaphoreType.DMA((ctx_count,))
    b_sems = pltpu.SemaphoreType.DMA((wa_count,))
    return pl.pallas_call(
        functools.partial(small_sum_kernel, ctx_count, wa_count),
        out_shape=jax.ShapeDtypeStruct(inner[1:], WIDE),
        in_specs=[pl.BlockSpec(memory_space=pltpu.VMEM)],
        out_specs=pl.BlockSpec(memory_space=pltpu.VMEM),
        scratch_shapes=[
            pltpu.VMEM(parts.shape, WIDE),
            pltpu.VMEM(inner, WIDE),
            pltpu.VMEM(inner, WIDE),
            a_sems,
            a_sems,
            b_sems,
            b_sems,
        ],
        compiler_params=pltpu.CompilerParams(collective_id=1, has_side_effects=True),
        name="small_sum",
    )(parts)


def on_device(
    block_input,
    cotangent,
    pair_order,
    norm_gains,
    norm_biases,
    w_qkv,
    attn_bias,
    w_out,
    resid_biases,
    w_fc,
    fc_bias,
    w_proj,
):
    ctx_count = lax.axis_size("ctx")
    wa_count = lax.axis_size("wa")
    device_count = ctx_count * wa_count
    ctx_index = lax.axis_index("ctx")
    tokens = block_input[0].astype(WIDE)
    row_count, model_width = tokens.shape
    block = row_count // 2
    share = model_width // device_count
    hidden_share = fc_bias.shape[0]
    width = model_width // ctx_count
    hidden_width = hidden_share * wa_count
    depth = w_qkv.shape[0]

    blocks = jnp.stack([pair_order, 2 * ctx_count - 1 - pair_order], axis=1).reshape(-1)
    numbers = jnp.arange(2 * ctx_count, dtype=jnp.int32)
    where = jnp.sum(
        jnp.where(blocks[None, :] == numbers[:, None], numbers[None, :], 0), axis=1
    ).astype(jnp.int32)

    small = jnp.concatenate(
        [
            norm_gains.reshape(-1),
            norm_biases.reshape(-1),
            attn_bias.reshape(-1),
            resid_biases.reshape(-1),
            fc_bias,
        ]
    ).astype(WIDE)
    small_size = small.shape[0]
    padded = -(-small_size // 1024) * 1024
    small = jnp.pad(small, (0, padded - small_size)).reshape(-1, 128)
    small_all = small_gather(small).reshape(device_count, padded)[:, :small_size]

    def rows_of(part):
        piece = small_all[:, part * 2 * share : (part + 1) * 2 * share]
        return piece.reshape(device_count, 2, share).transpose(1, 0, 2).reshape(2, model_width)

    gains, shifts, qv_bias, out_bias = (rows_of(part) for part in range(4))
    qv_own = lax.dynamic_slice_in_dim(qv_bias, ctx_index * width, width, axis=1)
    fc_own = lax.dynamic_slice_in_dim(
        small_all[:, 8 * share :], ctx_index * wa_count, wa_count, axis=0
    ).reshape(hidden_width)

    qkv_cut = w_qkv.reshape(depth, 3, ctx_count, width).transpose(2, 0, 1, 3)
    qkv_cut = qkv_cut.reshape(ctx_count, depth, 3 * width)
    qkv_cut = lax.all_to_all(qkv_cut, "ctx", 0, 0, tiled=True)
    qkv_own = lax.all_gather(qkv_cut, "wa", axis=1, tiled=True).reshape(model_width, 3 * width)
    out_own = lax.all_gather(w_out, "wa", axis=0, tiled=True)
    fc_cut = w_fc.reshape(depth, ctx_count, hidden_width).transpose(1, 0, 2)
    fc_cut = lax.all_to_all(fc_cut, "ctx", 0, 0, tiled=True)
    fc_mat = lax.all_gather(fc_cut, "wa", axis=1, tiled=True).reshape(model_width, hidden_width)
    proj_own = lax.all_gather(w_proj, "wa", axis=0, tiled=True)

    first_normed, first_factor = normalize(tokens)
    first = gather_rows((first_normed * gains[0] + shifts[0]).astype(LOW))
    qkv_bias = jnp.concatenate([qv_own[0], jnp.zeros((width,), WIDE), qv_own[1]])
    qkv = (jnp.dot(first, qkv_own, preferred_element_type=WIDE) + qkv_bias).astype(LOW)
    attended, logs = attend(where, qkv, block)
    branch = scatter_rows(jnp.dot(attended, out_own, preferred_element_type=WIDE).astype(LOW))
    hidden = tokens + branch + out_bias[0]

    second_normed, second_factor = normalize(hidden)
    second = gather_rows((second_normed * gains[1] + shifts[1]).astype(LOW))
    pre_act = jnp.dot(second, fc_mat, preferred_element_type=WIDE) + fc_own
    activation, gelu_pull = jax.vjp(gelu_tanh, pre_act)
    activation_low = activation.astype(LOW)
    grad_out = cotangent[0]
    grad_wide = grad_out.astype(WIDE)
    grad_all = gather_rows(grad_out)
    act_grad = contract(grad_all, proj_own, 1, 1)
    pre_grad = gelu_pull(act_grad)[0].astype(LOW)
    second_grad = scatter_rows(contract(pre_grad, fc_mat, 1, 1).astype(LOW))
    output = (
        hidden
        + scatter_rows(jnp.dot(activation_low, proj_own, preferred_element_type=WIDE).astype(LOW))
        + out_bias[1]
    )

    proj_grad = contract(activation_low, grad_all, 0, 0).astype(LOW)
    proj_sum = lax.psum_scatter(proj_grad, "wa", scatter_dimension=0, tiled=True).astype(WIDE)
    fc_grad = contract(second, pre_grad, 0, 0).astype(LOW)
    fc_grad = fc_grad.reshape(ctx_count, wa_count * depth, hidden_width)
    fc_sum = lax.psum_scatter(fc_grad, "wa", scatter_dimension=1, tiled=True)
    fc_sum = lax.all_to_all(fc_sum, "ctx", 0, 0, tiled=True)
    fc_sum = fc_sum.transpose(1, 0, 2).reshape(depth, -1).astype(WIDE)
    fc_bias_grad = jnp.sum(pre_grad.astype(WIDE), axis=0)

    gain_two = jnp.sum(second_grad * second_normed, axis=0)
    shift_two = jnp.sum(second_grad, axis=0)
    hidden_grad = grad_wide + norm_back(second_grad * gains[1], second_normed, second_factor)
    branch_low = hidden_grad.astype(LOW)
    branch_grad = gather_rows(branch_low)
    attended_grad = contract(branch_grad, out_own, 1, 1).astype(LOW)
    qkv_grad = attend_back(where, qkv, attended, attended_grad, logs, block)
    first_grad = scatter_rows(contract(qkv_grad, qkv_own, 1, 1).astype(LOW))

    out_grad = contract(attended, branch_grad, 0, 0).astype(LOW)
    out_sum = lax.psum_scatter(out_grad, "wa", scatter_dimension=0, tiled=True).astype(WIDE)
    weight_grad = contract(first, qkv_grad, 0, 0).astype(LOW)
    weight_grad = weight_grad.reshape(ctx_count, wa_count * depth, 3 * width)
    qkv_sum = lax.psum_scatter(weight_grad, "wa", scatter_dimension=1, tiled=True)
    qkv_sum = lax.all_to_all(qkv_sum, "ctx", 0, 0, tiled=True)
    qkv_sum = qkv_sum.reshape(ctx_count, depth, 3, width).transpose(1, 2, 0, 3)
    qkv_sum = qkv_sum.reshape(depth, 3 * model_width).astype(WIDE)
    qkv_bias_grad = jnp.sum(qkv_grad.astype(WIDE), axis=0)

    gain_one = jnp.sum(first_grad * first_normed, axis=0)
    shift_one = jnp.sum(first_grad, axis=0)
    input_grad = hidden_grad + norm_back(first_grad * gains[0], first_normed, first_factor)

    own = (lax.broadcasted_iota(jnp.int32, (ctx_count, 1), 0) == ctx_index).astype(WIDE)

    def spread(row):
        return (own * row[None]).reshape(-1)

    pairs = [
        gain_one,
        gain_two,
        shift_one,
        shift_two,
        spread(qkv_bias_grad[:width]),
        spread(qkv_bias_grad[2 * width :]),
        jnp.sum(branch_low.astype(WIDE), axis=0),
        jnp.sum(grad_wide, axis=0),
    ]
    owned = jnp.concatenate(
        [row.reshape(device_count, share) for row in pairs]
        + [spread(fc_bias_grad).reshape(device_count, hidden_share)],
        axis=1,
    )
    owned = jnp.pad(owned, ((0, 0), (0, padded - small_size)))
    mine = small_sum(owned.reshape(ctx_count, wa_count, -1, 128)).reshape(-1)[:small_size]
    small_grads = [
        mine[part * 2 * share : (part + 1) * 2 * share].reshape(2, share) for part in range(4)
    ]
    return (
        output.astype(LOW)[None],
        input_grad[None],
        small_grads[0],
        small_grads[1],
        qkv_sum,
        small_grads[2],
        out_sum,
        small_grads[3],
        fc_sum,
        mine[8 * share :],
        proj_sum,
    )


def solution(mesh):
    rows = P("wa", "ctx", None)
    first_dim = P(BOTH, None)
    second_dim = P(None, BOTH)
    return jax.shard_map(
        on_device,
        mesh=mesh,
        in_specs=(
            rows,
            rows,
            P(),
            second_dim,
            second_dim,
            first_dim,
            second_dim,
            first_dim,
            second_dim,
            first_dim,
            P(BOTH),
            first_dim,
        ),
        out_specs=(
            rows,
            rows,
            second_dim,
            second_dim,
            first_dim,
            second_dim,
            first_dim,
            second_dim,
            first_dim,
            P(BOTH),
            first_dim,
        ),
        check_vma=False,
    )
```

```python
import functools

import jax
import jax.numpy as jnp
from jax import lax
from jax.experimental import pallas as pl
from jax.experimental.pallas import tpu as pltpu
from jax.sharding import PartitionSpec as P

HEAD_DIM = 64
EPSILON = 1e-05
TILE = 256
BOTH = ("ctx", "wa")
LOW = jnp.bfloat16
WIDE = jnp.float32
MESH = pl.DeviceIdType.MESH


def normalize(field):
    average = jnp.mean(field, axis=-1, keepdims=True)
    centred = field - average
    variance = jnp.mean(centred * centred, axis=-1, keepdims=True)
    factor = lax.rsqrt(variance + EPSILON)
    return (centred * factor, factor)


def norm_back(grad_normed, normed, factor):
    return factor * (
        grad_normed
        - jnp.mean(grad_normed, axis=-1, keepdims=True)
        - normed * jnp.mean(grad_normed * normed, axis=-1, keepdims=True)
    )


def gelu_tanh(field):
    return (
        0.5
        * field
        * (1.0 + jnp.tanh(0.7978845608028654 * (field + 0.044715 * field * field * field)))
    )


def contract(left, right, left_dim, right_dim):
    return lax.dot_general(
        left, right, (((left_dim,), (right_dim,)), ((), ())), preferred_element_type=WIDE
    )


def causal(shape):
    keys = lax.broadcasted_iota(jnp.int32, shape, 0)
    rows = lax.broadcasted_iota(jnp.int32, shape, 1)
    return keys <= rows


def unpack(where_ref, source_ref, targets, block, scales):
    count = source_ref.shape[0] // block
    heads = targets[0].shape[0]

    def one(index, carried):
        rows = source_ref[pl.ds(pl.multiple_of(where_ref[index] * block, block), block), :]
        place = pl.ds(pl.multiple_of(index * block, block), block)
        for part, (target, scale) in enumerate(zip(targets, scales)):
            for head in range(heads):
                start = (part * heads + head) * HEAD_DIM
                piece = rows[:, start : start + HEAD_DIM]
                if scale != 1.0:
                    piece = (piece.astype(WIDE) * scale).astype(LOW)
                target[head, place, :] = piece
        return carried

    lax.fori_loop(0, count, one, 0)


def attend_kernel(block, where_ref, qkv_ref, out_ref, log_ref, q_s, k_s, v_s):
    step = pl.program_id(0)
    heads = q_s.shape[0]

    @pl.when(step == 0)
    def _():
        unpack(where_ref, qkv_ref, (q_s, k_s, v_s), block, (0.125, 1.0, 1.0))

    here = pl.ds(pl.multiple_of(step * TILE, TILE), TILE)
    queries = [q_s[head, here, :] for head in range(heads)]

    def visit(keys_at, state, masked):
        out = []
        for head in range(heads):
            top, total, summed = state[head]
            scores = contract(k_s[head, keys_at, :], queries[head], 1, 1)
            if masked:
                scores = jnp.where(causal(scores.shape), scores, -1e30)
            new_top = jnp.maximum(top, jnp.max(scores, axis=0, keepdims=True))
            weights = jnp.exp(scores - new_top)
            shrink = jnp.exp(top - new_top)
            total = total * shrink + jnp.sum(weights, axis=0, keepdims=True)
            summed = summed * shrink + contract(
                v_s[head, keys_at, :], weights.astype(LOW), 0, 0
            )
            out.append((new_top, total, summed))
        return tuple(out)

    start = tuple(
        (
            jnp.full((1, TILE), -1e30, WIDE),
            jnp.zeros((1, TILE), WIDE),
            jnp.zeros((HEAD_DIM, TILE), WIDE),
        )
        for _ in range(heads)
    )
    state = lax.fori_loop(
        0,
        step,
        lambda j, carried: visit(pl.ds(pl.multiple_of(j * TILE, TILE), TILE), carried, False),
        start,
    )
    state = visit(here, state, True)
    pieces = []
    for head in range(heads):
        top, total, summed = state[head]
        log_ref[step, head : head + 1, :] = top + jnp.log(total)
        pieces.append((summed / total).T)
    rows = jnp.concatenate(pieces, axis=1).astype(LOW) if heads > 1 else pieces[0].astype(LOW)
    per = TILE // block
    for part in range(per):
        place = pl.multiple_of(where_ref[step * per + part] * block, block)
        out_ref[pl.ds(place, block), :] = rows[part * block : (part + 1) * block, :]


def attend(where, qkv, block):
    rows, width = qkv.shape[0], qkv.shape[1] // 3
    heads = width // HEAD_DIM
    tiles = rows // TILE
    held = pltpu.VMEM((heads, rows, HEAD_DIM), LOW)
    return pl.pallas_call(
        functools.partial(attend_kernel, block),
        grid=(tiles,),
        out_shape=(
            jax.ShapeDtypeStruct((rows, width), LOW),
            jax.ShapeDtypeStruct((tiles, heads, TILE), WIDE),
        ),
        in_specs=[
            pl.BlockSpec(memory_space=pltpu.SMEM),
            pl.BlockSpec((rows, 3 * width), lambda i: (0, 0)),
        ],
        out_specs=(
            pl.BlockSpec((rows, width), lambda i: (0, 0)),
            pl.BlockSpec((tiles, heads, TILE), lambda i: (0, 0, 0)),
        ),
        scratch_shapes=[held, held, held],
        compiler_params=pltpu.CompilerParams(vmem_limit_bytes=48 << 20),
        cost_estimate=pl.CostEstimate(
            flops=2 * rows * rows * 2 * width,
            bytes_accessed=rows * width * 8,
            transcendentals=rows * rows * heads // 2,
        ),
        name="attend",
    )(where, qkv)


def attend_back_kernel(
    block,
    where_ref,
    qkv_ref,
    attended_ref,
    grad_ref,
    log_ref,
    out_ref,
    q_s,
    k_s,
    v_s,
    a_s,
    g_s,
    dq_s,
    delta_s,
):
    step = pl.program_id(0)
    tiles = pl.num_programs(0)
    heads = q_s.shape[0]
    width = heads * HEAD_DIM

    @pl.when(step == 0)
    def _():
        unpack(where_ref, qkv_ref, (q_s, k_s, v_s), block, (0.125, 1.0, 1.0))
        unpack(where_ref, attended_ref, (a_s,), block, (1.0,))
        unpack(where_ref, grad_ref, (g_s,), block, (1.0,))
        dq_s[...] = jnp.zeros_like(dq_s)

        def one(index, carried):
            place = pl.ds(pl.multiple_of(index * TILE, TILE), TILE)
            for head in range(heads):
                product = a_s[head, place, :].astype(WIDE) * g_s[head, place, :].astype(WIDE)
                delta_s[index, head : head + 1, :] = jnp.sum(product.T, axis=0, keepdims=True)
            return carried

        lax.fori_loop(0, delta_s.shape[0], one, 0)

    here = pl.ds(pl.multiple_of(step * TILE, TILE), TILE)
    keys = [k_s[head, here, :] for head in range(heads)]
    values = [v_s[head, here, :] for head in range(heads)]

    def visit(index, state, masked):
        place = pl.ds(pl.multiple_of(index * TILE, TILE), TILE)
        out = []
        for head in range(heads):
            dk, dv = state[head]
            queries = q_s[head, place, :]
            grads = g_s[head, place, :]
            scores = contract(keys[head], queries, 1, 1)
            if masked:
                scores = jnp.where(causal(scores.shape), scores, -1e30)
            weights = jnp.exp(scores - log_ref[index, head : head + 1, :])
            pulled = contract(values[head], grads, 1, 1)
            score_grad = (weights * (pulled - delta_s[index, head : head + 1, :])).astype(LOW)
            dv = dv + contract(weights.astype(LOW), grads, 1, 0)
            dk = dk + contract(score_grad, queries, 1, 0)
            dq_s[head, place, :] += contract(score_grad, keys[head], 0, 0)
            out.append((dk, dv))
        return tuple(out)

    zero = jnp.zeros((TILE, HEAD_DIM), WIDE)
    state = visit(step, tuple((zero, zero) for _ in range(heads)), True)
    state = lax.fori_loop(step + 1, tiles, lambda i, carried: visit(i, carried, False), state)
    pieces = [dq_s[head, here, :] * 0.125 for head in range(heads)]
    pieces += [state[head][0] for head in range(heads)]
    pieces += [state[head][1] for head in range(heads)]
    rows = jnp.concatenate(pieces, axis=1).astype(LOW)
    per = TILE // block
    for part in range(per):
        place = pl.multiple_of(where_ref[step * per + part] * block, block)
        out_ref[pl.ds(place, block), :] = rows[part * block : (part + 1) * block, :]


def attend_back(where, qkv, attended, grad, logs, block):
    rows, width = attended.shape
    heads = width // HEAD_DIM
    tiles = rows // TILE
    held = pltpu.VMEM((heads, rows, HEAD_DIM), LOW)

    def whole(*shape):
        return pl.BlockSpec(shape, lambda i: (0,) * len(shape))

    return pl.pallas_call(
        functools.partial(attend_back_kernel, block),
        grid=(tiles,),
        out_shape=jax.ShapeDtypeStruct((rows, 3 * width), LOW),
        in_specs=[
            pl.BlockSpec(memory_space=pltpu.SMEM),
            whole(rows, 3 * width),
            whole(rows, width),
            whole(rows, width),
            whole(tiles, heads, TILE),
        ],
        out_specs=whole(rows, 3 * width),
        scratch_shapes=[
            held,
            held,
            held,
            held,
            held,
            pltpu.VMEM((heads, rows, HEAD_DIM), WIDE),
            pltpu.VMEM((tiles, heads, TILE), WIDE),
        ],
        compiler_params=pltpu.CompilerParams(vmem_limit_bytes=56 << 20),
        cost_estimate=pl.CostEstimate(
            flops=5 * rows * rows * 2 * width,
            bytes_accessed=rows * width * 16,
            transcendentals=rows * rows * heads // 2,
        ),
        name="attend_back",
    )(where, qkv, attended, grad, logs)


def gather_rows(rows):
    return lax.all_gather(rows, "ctx", axis=0, tiled=True)


def greet(partners):
    barrier = pltpu.get_barrier_semaphore()
    for partner in partners:
        pl.semaphore_signal(barrier, inc=1, device_id=partner, device_id_type=MESH)
    pl.semaphore_wait(barrier, len(partners))


def remote(source, target, send, receive, partner):
    return pltpu.make_async_remote_copy(
        src_ref=source,
        dst_ref=target,
        send_sem=send,
        recv_sem=receive,
        device_id=partner,
        device_id_type=MESH,
    )


def scatter_kernel(
    count,
    partial_ref,
    out_ref,
    held,
    near,
    leaving,
    far,
    load_sem,
    near_send,
    near_recv,
    far_send,
    far_recv,
):
    chips = count // 2
    me = lax.axis_index("ctx")
    chip, core = me // 2, me % 2
    sibling = {"ctx": 2 * chip + 1 - core}
    places = [(chip + k) % chips for k in range(chips)]
    peers = [{"ctx": 2 * place + core} for place in places]
    loads, nears = {}, {}
    order = list(range(1, chips)) + [0]
    for k in order:
        loads[k] = pltpu.make_async_copy(
            partial_ref.at[2 * places[k] + core], held.at[k], load_sem.at[k]
        )
        loads[k].start()
    greet([sibling] + peers[1:])
    for k in order:
        nears[k] = remote(
            partial_ref.at[2 * places[k] + 1 - core],
            near.at[k],
            near_send.at[k],
            near_recv.at[k],
            sibling,
        )
        nears[k].start()
    fars = {}
    for k in range(1, chips):
        loads[k].wait()
        nears[k].wait_recv()
        leaving[k] = (held[k].astype(WIDE) + near[k].astype(WIDE)).astype(LOW)
        fars[k] = remote(
            leaving.at[k], far.at[chips - k], far_send.at[k], far_recv.at[chips - k], peers[k]
        )
        fars[k].start()
    loads[0].wait()
    nears[0].wait_recv()
    out_ref[...] = held[0].astype(WIDE) + near[0].astype(WIDE)
    for k in range(1, chips):
        fars[k].wait_recv()
        out_ref[...] += far[chips - k].astype(WIDE)
    for k in order:
        nears[k].wait_send()
    for k in range(1, chips):
        fars[k].wait_send()


def scatter_rows(partial):
    count = lax.axis_size("ctx")
    chips = count // 2
    rows, columns = partial.shape[0] // count, partial.shape[1]
    slots = pltpu.VMEM((chips, rows, columns), LOW)
    sems = pltpu.SemaphoreType.DMA((chips,))
    return pl.pallas_call(
        functools.partial(scatter_kernel, count),
        out_shape=jax.ShapeDtypeStruct((rows, columns), WIDE),
        in_specs=[pl.BlockSpec(memory_space=pl.ANY)],
        out_specs=pl.BlockSpec(memory_space=pltpu.VMEM),
        scratch_shapes=[slots] * 4 + [sems] * 5,
        compiler_params=pltpu.CompilerParams(
            collective_id=2, has_side_effects=True, vmem_limit_bytes=40 << 20
        ),
        cost_estimate=pl.CostEstimate(
            flops=count * rows * columns,
            bytes_accessed=40 * count * rows * columns,
            transcendentals=0,
        ),
        name="scatter_rows",
    )(partial.reshape(count, rows, columns))


def small_gather_kernel(ctx_count, wa_count, in_ref, out_ref, a_send, a_recv, b_send, b_recv):
    ctx, wa = lax.axis_index("ctx"), lax.axis_index("wa")
    along = [{"wa": (wa + k) % wa_count} for k in range(1, wa_count)]
    across = [{"ctx": (ctx + k) % ctx_count} for k in range(1, ctx_count)]
    greet(along + across)
    out_ref[ctx, wa] = in_ref[...]
    copies = [
        remote(in_ref, out_ref.at[ctx, wa], a_send.at[k], a_recv.at[k], partner)
        for k, partner in enumerate(along)
    ]
    for copy in copies:
        copy.start()
    for copy in copies:
        copy.wait()
    copies = [
        remote(out_ref.at[ctx], out_ref.at[ctx], b_send.at[k], b_recv.at[k], partner)
        for k, partner in enumerate(across)
    ]
    for copy in copies:
        copy.start()
    for copy in copies:
        copy.wait()


def small_gather(rows):
    ctx_count, wa_count = lax.axis_size("ctx"), lax.axis_size("wa")
    a_sems = pltpu.SemaphoreType.DMA((wa_count - 1,))
    b_sems = pltpu.SemaphoreType.DMA((ctx_count - 1,))
    return pl.pallas_call(
        functools.partial(small_gather_kernel, ctx_count, wa_count),
        out_shape=jax.ShapeDtypeStruct((ctx_count, wa_count) + rows.shape, WIDE),
        in_specs=[pl.BlockSpec(memory_space=pltpu.VMEM)],
        out_specs=pl.BlockSpec(memory_space=pltpu.VMEM),
        scratch_shapes=[a_sems, a_sems, b_sems, b_sems],
        compiler_params=pltpu.CompilerParams(collective_id=0, has_side_effects=True),
        name="small_gather",
    )(rows)


def small_sum_kernel(
    ctx_count, wa_count, in_ref, out_ref, a_s, mid_s, b_s, a_send, a_recv, b_send, b_recv
):
    ctx, wa = lax.axis_index("ctx"), lax.axis_index("wa")
    greet(
        [{"wa": (wa + k) % wa_count} for k in range(1, wa_count)]
        + [{"ctx": (ctx + k) % ctx_count} for k in range(1, ctx_count)]
    )
    copies = []
    for k in range(1, ctx_count):
        place = (ctx + k) % ctx_count
        copies.append(
            remote(in_ref.at[place], a_s.at[k], a_send.at[k], a_recv.at[k], {"ctx": place})
        )
        copies[-1].start()
    total = in_ref[ctx]
    for k in range(1, ctx_count):
        copies[k - 1].wait()
        total = total + a_s[k]
    mid_s[...] = total
    copies = []
    for k in range(1, wa_count):
        place = (wa + k) % wa_count
        copies.append(
            remote(mid_s.at[place], b_s.at[k], b_send.at[k], b_recv.at[k], {"wa": place})
        )
        copies[-1].start()
    total = mid_s[wa]
    for k in range(1, wa_count):
        copies[k - 1].wait()
        total = total + b_s[k]
    out_ref[...] = total


def small_sum(parts):
    ctx_count, wa_count = parts.shape[:2]
    inner = parts.shape[1:]
    a_sems = pltpu.SemaphoreType.DMA((ctx_count,))
    b_sems = pltpu.SemaphoreType.DMA((wa_count,))
    return pl.pallas_call(
        functools.partial(small_sum_kernel, ctx_count, wa_count),
        out_shape=jax.ShapeDtypeStruct(inner[1:], WIDE),
        in_specs=[pl.BlockSpec(memory_space=pltpu.VMEM)],
        out_specs=pl.BlockSpec(memory_space=pltpu.VMEM),
        scratch_shapes=[
            pltpu.VMEM(parts.shape, WIDE),
            pltpu.VMEM(inner, WIDE),
            pltpu.VMEM(inner, WIDE),
            a_sems,
            a_sems,
            b_sems,
            b_sems,
        ],
        compiler_params=pltpu.CompilerParams(collective_id=1, has_side_effects=True),
        name="small_sum",
    )(parts)


def on_device(
    block_input,
    cotangent,
    pair_order,
    norm_gains,
    norm_biases,
    w_qkv,
    attn_bias,
    w_out,
    resid_biases,
    w_fc,
    fc_bias,
    w_proj,
):
    ctx_count = lax.axis_size("ctx")
    wa_count = lax.axis_size("wa")
    device_count = ctx_count * wa_count
    ctx_index = lax.axis_index("ctx")
    tokens = block_input[0].astype(WIDE)
    row_count, model_width = tokens.shape
    block = row_count // 2
    share = model_width // device_count
    hidden_share = fc_bias.shape[0]
    width = model_width // ctx_count
    hidden_width = hidden_share * wa_count
    depth = w_qkv.shape[0]

    blocks = jnp.stack([pair_order, 2 * ctx_count - 1 - pair_order], axis=1).reshape(-1)
    numbers = jnp.arange(2 * ctx_count, dtype=jnp.int32)
    where = jnp.sum(
        jnp.where(blocks[None, :] == numbers[:, None], numbers[None, :], 0), axis=1
    ).astype(jnp.int32)

    small = jnp.concatenate(
        [
            norm_gains.reshape(-1),
            norm_biases.reshape(-1),
            attn_bias.reshape(-1),
            resid_biases.reshape(-1),
            fc_bias,
        ]
    ).astype(WIDE)
    small_size = small.shape[0]
    padded = -(-small_size // 1024) * 1024
    small = jnp.pad(small, (0, padded - small_size)).reshape(-1, 128)
    small_all = small_gather(small).reshape(device_count, padded)[:, :small_size]

    def rows_of(part):
        piece = small_all[:, part * 2 * share : (part + 1) * 2 * share]
        return piece.reshape(device_count, 2, share).transpose(1, 0, 2).reshape(2, model_width)

    gains, shifts, qv_bias, out_bias = (rows_of(part) for part in range(4))
    qv_own = lax.dynamic_slice_in_dim(qv_bias, ctx_index * width, width, axis=1)
    fc_own = lax.dynamic_slice_in_dim(
        small_all[:, 8 * share :], ctx_index * wa_count, wa_count, axis=0
    ).reshape(hidden_width)

    qkv_cut = w_qkv.reshape(depth, 3, ctx_count, width).transpose(2, 0, 1, 3)
    qkv_cut = qkv_cut.reshape(ctx_count, depth, 3 * width)
    qkv_cut = lax.all_to_all(qkv_cut, "ctx", 0, 0, tiled=True)
    qkv_own = lax.all_gather(qkv_cut, "wa", axis=1, tiled=True).reshape(model_width, 3 * width)
    out_own = lax.all_gather(w_out, "wa", axis=0, tiled=True)
    fc_cut = w_fc.reshape(depth, ctx_count, hidden_width).transpose(1, 0, 2)
    fc_cut = lax.all_to_all(fc_cut, "ctx", 0, 0, tiled=True)
    fc_mat = lax.all_gather(fc_cut, "wa", axis=1, tiled=True).reshape(model_width, hidden_width)
    proj_own = lax.all_gather(w_proj, "wa", axis=0, tiled=True)

    first_normed, first_factor = normalize(tokens)
    first = gather_rows((first_normed * gains[0] + shifts[0]).astype(LOW))
    qkv_bias = jnp.concatenate([qv_own[0], jnp.zeros((width,), WIDE), qv_own[1]])
    qkv = (jnp.dot(first, qkv_own, preferred_element_type=WIDE) + qkv_bias).astype(LOW)
    attended, logs = attend(where, qkv, block)
    branch = jnp.dot(attended, out_own, preferred_element_type=WIDE).astype(LOW)
    branch, grad_all = lax.optimization_barrier((branch, gather_rows(cotangent[0])))
    branch = scatter_rows(branch)
    branch, proj_own, fc_mat = lax.optimization_barrier((branch, proj_own, fc_mat))
    hidden = tokens + branch + out_bias[0]

    second_normed, second_factor = normalize(hidden)
    second = gather_rows((second_normed * gains[1] + shifts[1]).astype(LOW))
    pre_act = jnp.dot(second, fc_mat, preferred_element_type=WIDE) + fc_own
    activation, gelu_pull = jax.vjp(gelu_tanh, pre_act)
    activation_low = activation.astype(LOW)
    grad_out = cotangent[0]
    grad_wide = grad_out.astype(WIDE)
    act_grad = contract(grad_all, proj_own, 1, 1)
    pre_grad = gelu_pull(act_grad)[0].astype(LOW)
    second_grad = scatter_rows(contract(pre_grad, fc_mat, 1, 1).astype(LOW))
    output = (
        hidden
        + scatter_rows(jnp.dot(activation_low, proj_own, preferred_element_type=WIDE).astype(LOW))
        + out_bias[1]
    )

    proj_grad = contract(activation_low, grad_all, 0, 0).astype(LOW)
    proj_sum = lax.psum_scatter(proj_grad, "wa", scatter_dimension=0, tiled=True).astype(WIDE)
    fc_grad = contract(second, pre_grad, 0, 0).astype(LOW)
    fc_grad = fc_grad.reshape(ctx_count, wa_count * depth, hidden_width)
    fc_sum = lax.psum_scatter(fc_grad, "wa", scatter_dimension=1, tiled=True)
    fc_sum = lax.all_to_all(fc_sum, "ctx", 0, 0, tiled=True)
    fc_sum = fc_sum.transpose(1, 0, 2).reshape(depth, -1).astype(WIDE)
    fc_bias_grad = jnp.sum(pre_grad.astype(WIDE), axis=0)

    gain_two = jnp.sum(second_grad * second_normed, axis=0)
    shift_two = jnp.sum(second_grad, axis=0)
    hidden_grad = grad_wide + norm_back(second_grad * gains[1], second_normed, second_factor)
    branch_low = hidden_grad.astype(LOW)
    branch_grad = gather_rows(branch_low)
    attended_grad = contract(branch_grad, out_own, 1, 1).astype(LOW)
    qkv_grad = attend_back(where, qkv, attended, attended_grad, logs, block)
    first_grad = scatter_rows(contract(qkv_grad, qkv_own, 1, 1).astype(LOW))

    out_grad = contract(attended, branch_grad, 0, 0).astype(LOW)
    out_sum = lax.psum_scatter(out_grad, "wa", scatter_dimension=0, tiled=True).astype(WIDE)
    weight_grad = contract(first, qkv_grad, 0, 0).astype(LOW)
    weight_grad = weight_grad.reshape(ctx_count, wa_count * depth, 3 * width)
    qkv_sum = lax.psum_scatter(weight_grad, "wa", scatter_dimension=1, tiled=True)
    qkv_sum = lax.all_to_all(qkv_sum, "ctx", 0, 0, tiled=True)
    qkv_sum = qkv_sum.reshape(ctx_count, depth, 3, width).transpose(1, 2, 0, 3)
    qkv_sum = qkv_sum.reshape(depth, 3 * model_width).astype(WIDE)
    qkv_bias_grad = jnp.sum(qkv_grad.astype(WIDE), axis=0)

    gain_one = jnp.sum(first_grad * first_normed, axis=0)
    shift_one = jnp.sum(first_grad, axis=0)
    input_grad = hidden_grad + norm_back(first_grad * gains[0], first_normed, first_factor)

    own = (lax.broadcasted_iota(jnp.int32, (ctx_count, 1), 0) == ctx_index).astype(WIDE)

    def spread(row):
        return (own * row[None]).reshape(-1)

    pairs = [
        gain_one,
        gain_two,
        shift_one,
        shift_two,
        spread(qkv_bias_grad[:width]),
        spread(qkv_bias_grad[2 * width :]),
        jnp.sum(branch_low.astype(WIDE), axis=0),
        jnp.sum(grad_wide, axis=0),
    ]
    owned = jnp.concatenate(
        [row.reshape(device_count, share) for row in pairs]
        + [spread(fc_bias_grad).reshape(device_count, hidden_share)],
        axis=1,
    )
    owned = jnp.pad(owned, ((0, 0), (0, padded - small_size)))
    mine = small_sum(owned.reshape(ctx_count, wa_count, -1, 128)).reshape(-1)[:small_size]
    small_grads = [
        mine[part * 2 * share : (part + 1) * 2 * share].reshape(2, share) for part in range(4)
    ]
    return (
        output.astype(LOW)[None],
        input_grad[None],
        small_grads[0],
        small_grads[1],
        qkv_sum,
        small_grads[2],
        out_sum,
        small_grads[3],
        fc_sum,
        mine[8 * share :],
        proj_sum,
    )


def solution(mesh):
    rows = P("wa", "ctx", None)
    first_dim = P(BOTH, None)
    second_dim = P(None, BOTH)
    return jax.shard_map(
        on_device,
        mesh=mesh,
        in_specs=(
            rows,
            rows,
            P(),
            second_dim,
            second_dim,
            first_dim,
            second_dim,
            first_dim,
            second_dim,
            first_dim,
            P(BOTH),
            first_dim,
        ),
        out_specs=(
            rows,
            rows,
            second_dim,
            second_dim,
            first_dim,
            second_dim,
            first_dim,
            second_dim,
            first_dim,
            P(BOTH),
            first_dim,
        ),
        check_vma=False,
    )
```
